256 devices in a mesh: row: 8 (over y, core), col: 32 (over x, z).
Axes of the slice: x: 4, y: 4, z: 8, core: 2. Of those that a mesh axis runs over, the one named last changes fastest.
Arguments:
- tokens: bfloat16 [1024, 8192], P('col', 'row'), may hold values from -6 to 6
- gate_weight: bfloat16 [8192, 28672], P('row', 'col'), may hold values from -0.0625 to 0.0625
- up_weight: bfloat16 [8192, 28672], P('row', 'col'), may hold values from -0.0625 to 0.0625
- down_weight: bfloat16 [28672, 8192], P('col', 'row'), may hold values from -0.03125 to 0.03125
- out_grad: bfloat16 [1024, 8192], P('col', 'row'), may hold values from -0.1875 to 0.1875
Outputs:
- mixed: bfloat16 [1024, 8192], P('col', 'row')
- down_grad: float32 [28672, 8192], P('col', 'row')
The draws below stay inside these ranges and needn't reach their ends.
All inputs are finite; a program needn't handle non-finite values.
Results may differ from the reference program's by a relative error of at most 0.0049.
Values may be sent and summed in bfloat16 or wider, within the bound.
A program may use at most 64 MiB of HBM per device.

```python
import jax
import jax.numpy as jnp

D = 8192
FF = 28672
TOKENS = 1024


def steps_of(key, dims, pieces, smallest, top_value):
    factor_of, own = 1.0, jax.random.fold_in(key, 6)
    for axis_at, blocks in pieces:
        heights = jnp.exp(jax.random.uniform(jax.random.fold_in(own, axis_at), (blocks,), jnp.float32, smallest / len(pieces), top_value / len(pieces)))
        factor_of = factor_of * jnp.repeat(heights, dims[axis_at] // blocks).reshape([-1 if axis == axis_at else 1 for axis in range(len(dims))])
    return factor_of


def centred(key, extent, spread, limit, shards=(), dtype=jnp.bfloat16):
    level = steps_of(key, extent, shards, -0.22, 0.18) if shards else 1.0
    values = jax.random.normal(key, extent, jnp.float32) * spread * level
    return jnp.minimum(jnp.maximum(values, -limit), limit).astype(dtype)


def setup_inputs(seed: int = 0) -> dict:
    keys = jax.random.split(jax.random.key(seed), 6)
    tokens = centred(keys[0], (TOKENS, D), 1.0, 6.0, ((0, 32), (1, 8)))
    gate_weight = centred(keys[1], (D, FF), D ** -0.5, 0.0625, ((0, 8), (1, 32)))
    up_weight = centred(keys[2], (D, FF), D ** -0.5, 0.0625, ((0, 8), (1, 32)))
    down_weight = centred(keys[3], (FF, D), FF ** -0.5, 0.03125, ((0, 32), (1, 8)))
    out_grad = centred(keys[4], (TOKENS, D), (TOKENS ** -0.5), 0.1875, ((0, 32), (1, 8)))
    return {"tokens": tokens, "gate_weight": gate_weight, "up_weight": up_weight, "down_weight": down_weight, "out_grad": out_grad}


def reference(tokens, gate_weight, up_weight, down_weight, out_grad):
    gate = jnp.dot(tokens, gate_weight, preferred_element_type=jnp.float32)
    up = jnp.dot(tokens, up_weight, preferred_element_type=jnp.float32)
    hidden = (jax.nn.silu(gate) * up).astype(jnp.bfloat16)
    mixed = jnp.dot(hidden, down_weight, preferred_element_type=jnp.float32).astype(jnp.bfloat16)
    down_grad = jnp.dot(hidden.T, out_grad, preferred_element_type=jnp.float32)
    return mixed, down_grad
```

```python
import jax
import jax.numpy as jnp
from jax import lax
from jax.experimental import pallas as pl
from jax.experimental.pallas import tpu as pltpu
from jax.sharding import PartitionSpec as P

MESH = pl.DeviceIdType.MESH
BF16, F32 = jnp.bfloat16, jnp.float32
NX, NY, NZ = 4, 4, 8
OWN = 32
CHUNK = NX * OWN
PART = CHUNK // (2 * NY)


def kernel(
    tokens, gate_w, up_w, down_w, out_grad, mixed, down_grad,
    w, wd, tok, og, part, core_in, y_out, y_in, hid, hid_t, x_own, x_out, x_in, z_out, z_in, dg,
    w_sem, dg_sem,
    zt_s, zt_r, xt_s, xt_r, c1_s, c1_r, y1_s, y1_r, y2_s, y2_r, c2_s, c2_r, x2_s, x2_r, z2_s, z2_r, ox_s, ox_r, oz_s, oz_r,
):
    ff = gate_w.shape[1]
    row, col = lax.axis_index("row"), lax.axis_index("col")
    y, c, x, z = row // 2, row % 2, col // NZ, col % NZ

    def dev(px, py, pz, pc):
        return (py * 2 + pc, px * NZ + pz)

    x_peer = [dev((x + j) % NX, y, z, c) for j in range(NX)]
    y_peer = [dev(x, (y + j) % NY, z, c) for j in range(NY)]
    z_up, z_down = dev(x, y, (z + 1) % NZ, c), dev(x, y, (z + NZ - 1) % NZ, c)
    sibling = dev(x, y, z, 1 - c)

    def send(src, dst, ss, rs, to):
        return pltpu.make_async_remote_copy(
            src_ref=src, dst_ref=dst, send_sem=ss, recv_sem=rs, device_id=to, device_id_type=MESH)

    def arrived(dst, ss, rs):
        send(dst, dst, ss, rs, sibling).wait_recv()

    def sent(src, ss, rs):
        send(src, src, ss, rs, sibling).wait_send()

    loads = [
        pltpu.make_async_copy(gate_w, w.at[:, pl.ds(0, ff)], w_sem.at[0]),
        pltpu.make_async_copy(up_w, w.at[:, pl.ds(ff, ff)], w_sem.at[1]),
        pltpu.make_async_copy(down_w, wd, w_sem.at[2]),
    ]
    for load in loads:
        load.start()

    barrier = pltpu.get_barrier_semaphore()
    for j in range(1, NX):
        pl.semaphore_signal(barrier, inc=1, device_id=x_peer[j], device_id_type=MESH)
    for j in range(1, NY):
        pl.semaphore_signal(barrier, inc=1, device_id=y_peer[j], device_id_type=MESH)
    for j in range(1, NZ):
        pl.semaphore_signal(barrier, inc=1, device_id=dev(x, y, (z + j) % NZ, c), device_id_type=MESH)
    pl.semaphore_signal(barrier, inc=1, device_id=sibling, device_id_type=MESH)
    tok[0, x] = tokens[...]
    og[0, x] = out_grad[...]
    pl.semaphore_wait(barrier, NX + NY + NZ - 2)

    def tok_x(r):
        for j in (2, 1, 3):
            send(tok.at[r, x], tok.at[r, x], xt_s.at[r, j - 1], xt_r.at[r, j - 1], x_peer[j]).start()

    def tok_step(d):
        half = OWN // 2
        if d == 0:
            send(tok.at[0, x], tok.at[NZ - 1, x], zt_s.at[NZ - 1], zt_r.at[NZ - 1], z_up).start()
            send(tok.at[0, x], tok.at[1, x], zt_s.at[1], zt_r.at[1], z_down).start()
            tok_x(0)
        elif d < NZ // 2:
            e = NZ - d
            arrived(tok.at[d, x], zt_s.at[d], zt_r.at[d])
            if d < NZ // 2 - 1:
                send(tok.at[d, x], tok.at[d + 1, x], zt_s.at[d + 1], zt_r.at[d + 1], z_down).start()
            else:
                hi = pl.ds(half, half)
                send(tok.at[d, x, hi], tok.at[d + 1, x, hi], zt_s.at[0], zt_r.at[0], z_down).start()
            tok_x(d)
            arrived(tok.at[e, x], zt_s.at[e], zt_r.at[e])
            if d < NZ // 2 - 1:
                send(tok.at[e, x], tok.at[e - 1, x], zt_s.at[e - 1], zt_r.at[e - 1], z_up).start()
            else:
                lo = pl.ds(0, half)
                send(tok.at[e, x, lo], tok.at[e - 1, x, lo], zt_s.at[e - 1], zt_r.at[e - 1], z_up).start()
            tok_x(e)
        else:
            arrived(tok.at[d, x, pl.ds(0, half)], zt_s.at[d], zt_r.at[d])
            arrived(tok.at[d, x, pl.ds(half, half)], zt_s.at[0], zt_r.at[0])
            tok_x(d)

    def og_start():
        for j in (2, 1, 3):
            send(og.at[0, x], og.at[0, x], ox_s.at[j - 1], ox_r.at[j - 1], x_peer[j]).start()

    def og_step(d):
        half = NX // 2
        if d == 0:
            for j in range(1, NX):
                arrived(og.at[0, 0], ox_s.at[j - 1], ox_r.at[j - 1])
            send(og.at[0], og.at[NZ - 1], oz_s.at[NZ - 1], oz_r.at[NZ - 1], z_up).start()
            send(og.at[0], og.at[1], oz_s.at[1], oz_r.at[1], z_down).start()
        elif d < NZ // 2:
            e = NZ - d
            arrived(og.at[d], oz_s.at[d], oz_r.at[d])
            if d < NZ // 2 - 1:
                send(og.at[d], og.at[d + 1], oz_s.at[d + 1], oz_r.at[d + 1], z_down).start()
            else:
                hi = pl.ds(half, half)
                send(og.at[d, hi], og.at[d + 1, hi], oz_s.at[0], oz_r.at[0], z_down).start()
            arrived(og.at[e], oz_s.at[e], oz_r.at[e])
            if d < NZ // 2 - 1:
                send(og.at[e], og.at[e - 1], oz_s.at[e - 1], oz_r.at[e - 1], z_up).start()
            else:
                lo = pl.ds(0, half)
                send(og.at[e, lo], og.at[e - 1, lo], oz_s.at[e - 1], oz_r.at[e - 1], z_up).start()
        else:
            arrived(og.at[d, pl.ds(0, half)], oz_s.at[d], oz_r.at[d])
            arrived(og.at[d, pl.ds(half, half)], oz_s.at[0], oz_r.at[0])

    def slot(p):
        return jnp.where(p % 2 == 1, (p + 1) // 2, (NZ - p // 2) % NZ)

    def s1(p):
        r = slot(p)
        for j in range(1, NX):
            arrived(tok.at[r, 0], xt_s.at[r, j - 1], xt_r.at[r, j - 1])
        a = tok[r].reshape(CHUNK, tokens.shape[1])

        @pl.loop(0, w.shape[1] // 256)
        def _(n):
            cols = pl.ds(pl.multiple_of(n * 256, 256), 256)
            part[r, :, :, :, cols] = jnp.dot(a, w[:, cols], preferred_element_type=F32).reshape(2, NY, PART, 256)

        send(part.at[r, 1 - c], core_in.at[r], c1_s.at[r], c1_r.at[r], sibling).start()

    def s2(p):
        r = slot(p)
        arrived(core_in.at[r], c1_s.at[r], c1_r.at[r])
        for j in (2, 1, 3):
            to = (y + j) % NY
            y_out[r, j - 1] = (part[r, c, to] + core_in[r, to]).astype(BF16)
            send(y_out.at[r, j - 1], y_in.at[r, j - 1], y1_s.at[r, j - 1], y1_r.at[r, j - 1], y_peer[j]).start()

    def s3(p):
        r = slot(p)
        total = part[r, c, y] + core_in[r, y]
        for j in (1, 3, 2):
            arrived(y_in.at[r, j - 1], y1_s.at[r, j - 1], y1_r.at[r, j - 1])
            total = total + y_in[r, j - 1].astype(F32)
        gate, up = total[:, :ff], total[:, ff:]
        hid[r, c * NY + y] = (gate / (1.0 + jnp.exp(-gate)) * up).astype(BF16)
        mine = hid.at[r, c * NY + y]
        for j in (2, 1, 3):
            send(mine, mine, y2_s.at[r, j - 1], y2_r.at[r, j - 1], y_peer[j]).start()

    def s4(p):
        r = slot(p)
        for j in (1, 3, 2):
            arrived(hid.at[r, 0], y2_s.at[r, j - 1], y2_r.at[r, j - 1])
        mine = hid.at[r, pl.ds(c * NY, NY)]
        send(mine, mine, c2_s.at[r], c2_r.at[r], sibling).start()

    def s5(p):
        r = slot(p)
        arrived(hid.at[r, pl.ds(0, NY)], c2_s.at[r], c2_r.at[r])
        h = hid[r].reshape(CHUNK, ff)

        @pl.loop(0, wd.shape[1] // 256)
        def _(n):
            cols = pl.ds(pl.multiple_of(n * 256, 256), 256)
            out = jnp.dot(h, wd[:, cols], preferred_element_type=F32).reshape(NX, OWN, 256)
            x_own[r, :, :, cols] = out
            x_out[r, :, :, cols] = out.astype(BF16)

        for j in (2, 1, 3):
            send(x_out.at[r, (x + j) % NX], x_in.at[r, j - 1], x2_s.at[r, j - 1], x2_r.at[r, j - 1], x_peer[j]).start()
        hid_t[:, pl.ds(pl.multiple_of(r * CHUNK, CHUNK), CHUNK)] = h.T

    def s6(p):
        r = slot(p)
        total = x_own[r, x]
        for j in (1, 3, 2):
            arrived(x_in.at[r, j - 1], x2_s.at[r, j - 1], x2_r.at[r, j - 1])
            total = total + x_in[r, j - 1].astype(F32)

        @pl.when(r == 0)
        def _():
            x_own[0, x] = total

        @pl.when(r != 0)
        def _():
            z_out[r] = total.astype(BF16)
            send(z_out.at[r], z_in.at[r], z2_s.at[r], z2_r.at[r], dev(x, y, (z + r) % NZ, c)).start()

    def grad(n):
        cols = pl.ds(n * 256, 256)
        dg[:, cols] = jnp.dot(
            hid_t[...], og[:, :, :, cols].reshape(NZ * CHUNK, 256), preferred_element_type=F32)
        pltpu.make_async_copy(dg.at[:, cols], down_grad.at[:, cols], dg_sem.at[n]).start()

    tok_step(0)

    @pl.loop(0, 11)
    def _(t):
        for d in range(1, NZ // 2 + 1):
            @pl.when(t == d - 1)
            def _():
                if d == 1:
                    loads[0].wait()
                    loads[1].wait()
                if d == 3:
                    loads[2].wait()
                tok_step(d)
                if d == 2:
                    og_start()

        @pl.when(t < NZ)
        def _():
            s1(t)

        @pl.when((t >= 3) & (t < NZ + 3))
        def _():
            s4(t - 3)

        @pl.when((t >= 2) & (t < NZ + 2))
        def _():
            s3(t - 2)

        @pl.when(t >= 6)
        def _():
            s6(t - 6)

        @pl.when((t >= 3) & (t < NZ + 3))
        def _():
            s5(t - 3)

        @pl.when(t < NZ)
        def _():
            s2(t)

        for d, at in enumerate((2, 4, 6, 8, 10)):
            @pl.when(t == at)
            def _():
                og_step(d)

    s6(jnp.int32(5))
    grad(0)
    grad(1)
    s6(jnp.int32(6))
    grad(2)
    grad(3)
    s6(jnp.int32(7))

    total = x_own[0, x]
    for r in (4, 3, 5, 2, 6, 1, 7):
        arrived(z_in.at[r], z2_s.at[r], z2_r.at[r])
        total = total + z_in[r].astype(F32)
    mixed[...] = total.astype(BF16)

    half = OWN // 2
    for r in range(NZ):
        if r in (0, NZ // 2):
            sent(tok.at[0, 0, pl.ds(0, half)], zt_s.at[r], zt_r.at[r])
            sent(og.at[0, pl.ds(0, NX // 2)], oz_s.at[r], oz_r.at[r])
        else:
            sent(tok.at[0, 0], zt_s.at[r], zt_r.at[r])
            sent(og.at[0], oz_s.at[r], oz_r.at[r])

    for j in range(NX - 1):
        sent(og.at[0, 0], ox_s.at[j], ox_r.at[j])

    @pl.loop(0, NZ)
    def _(r):
        sent(part.at[0, 0], c1_s.at[r], c1_r.at[r])
        sent(hid.at[0, pl.ds(0, NY)], c2_s.at[r], c2_r.at[r])
        for j in range(NX - 1):
            sent(tok.at[0, 0], xt_s.at[r, j], xt_r.at[r, j])
            sent(x_out.at[0, 0], x2_s.at[r, j], x2_r.at[r, j])
        for j in range(NY - 1):
            sent(y_out.at[0, 0], y1_s.at[r, j], y1_r.at[r, j])
            sent(hid.at[0, 0], y2_s.at[r, j], y2_r.at[r, j])

        @pl.when(r != 0)
        def _():
            sent(z_out.at[0], z2_s.at[r], z2_r.at[r])

    for n in range(dg.shape[1] // 256):
        cols = pl.ds(n * 256, 256)
        pltpu.make_async_copy(dg.at[:, cols], down_grad.at[:, cols], dg_sem.at[n]).wait()


def local(tokens, gate_w, up_w, down_w, out_grad):
    d, ff = gate_w.shape
    dma = pltpu.SemaphoreType.DMA
    vmem, hbm = pl.BlockSpec(memory_space=pltpu.VMEM), pl.BlockSpec(memory_space=pl.ANY)
    pair = lambda *shape: [dma(shape), dma(shape)]
    return pl.pallas_call(
        kernel,
        out_shape=(
            jax.ShapeDtypeStruct((OWN, d), BF16),
            jax.ShapeDtypeStruct((ff, d), F32),
        ),
        in_specs=[vmem, hbm, hbm, hbm, vmem],
        out_specs=(vmem, hbm),
        scratch_shapes=[
            pltpu.VMEM((d, 2 * ff), BF16),
            pltpu.VMEM((ff, d), BF16),
            pltpu.VMEM((NZ, NX, OWN, d), BF16),
            pltpu.VMEM((NZ, NX, OWN, d), BF16),
            pltpu.VMEM((NZ, 2, NY, PART, 2 * ff), F32),
            pltpu.VMEM((NZ, NY, PART, 2 * ff), F32),
            pltpu.VMEM((NZ, NY - 1, PART, 2 * ff), BF16),
            pltpu.VMEM((NZ, NY - 1, PART, 2 * ff), BF16),
            pltpu.VMEM((NZ, 2 * NY, PART, ff), BF16),
            pltpu.VMEM((ff, NZ * CHUNK), BF16),
            pltpu.VMEM((NZ, NX, OWN, d), F32),
            pltpu.VMEM((NZ, NX, OWN, d), BF16),
            pltpu.VMEM((NZ, NX - 1, OWN, d), BF16),
            pltpu.VMEM((NZ, OWN, d), BF16),
            pltpu.VMEM((NZ, OWN, d), BF16),
            pltpu.VMEM((ff, d), F32),
            dma((3,)),
            dma((d // 256,)),
            *pair(NZ), *pair(NZ, NX - 1), *pair(NZ), *pair(NZ, NY - 1), *pair(NZ, NY - 1),
            *pair(NZ), *pair(NZ, NX - 1), *pair(NZ), *pair(NX - 1), *pair(NZ),
        ],
        compiler_params=pltpu.CompilerParams(
            collective_id=0, has_side_effects=True, vmem_limit_bytes=56 * 2**20),
        cost_estimate=pl.CostEstimate(flops=7_600_000_000, bytes_accessed=10_000_000, transcendentals=120_000),
    )(tokens, gate_w, up_w, down_w, out_grad)


def solution(mesh):
    return jax.shard_map(
        local,
        mesh=mesh,
        in_specs=(P("col", "row"), P("row", "col"), P("row", "col"), P("col", "row"), P("col", "row")),
        out_specs=(P("col", "row"), P("col", "row")),
        check_vma=False,
    )
```

```python
import jax
import jax.numpy as jnp
from jax import lax
from jax.experimental import pallas as pl
from jax.experimental.pallas import tpu as pltpu
from jax.sharding import PartitionSpec as P

MESH = pl.DeviceIdType.MESH
BF16, F32 = jnp.bfloat16, jnp.float32
NX, NY, NZ = 4, 4, 8
OWN = 32
CHUNK = NX * OWN
PART = CHUNK // (2 * NY)


ORDER = (0, 4, 3, 5, 2, 6, 7, 1)
FAR_FIRST = (4, 3, 5, 2, 6, 1, 7)
CUT = None


def schedule():
    return (
        ("tokr", 0), ("og_start",), ("s1", 0), ("tokr", 4), ("s2", 0), ("og", 0), ("tokr", 3), ("tokr", 5),
        ("s1", 1), ("tokr", 2), ("tokr", 6), ("tokr", 1), ("tokr", 7), ("s3", 0), ("s2", 1), ("s1", 2), ("s4", 0),
        ("s2", 2), ("s1", 3), ("s5", 0), ("og", 1), ("s3", 1), ("s2", 3), ("s1", 4), ("s3", 2), ("s1", 5),
        ("s2", 4), ("s4", 1), ("s2", 5), ("s5", 1), ("s3", 3), ("s4", 2), ("og", 2), ("s1", 6), ("s5", 2),
        ("s3", 4), ("s1", 7), ("s2", 6), ("s6", 0), ("s3", 5), ("s2", 7), ("s4", 3), ("s6", 1), ("s5", 3),
        ("s4", 4), ("og", 3), ("s5", 4), ("s3", 6), ("s6", 2), ("s4", 5), ("s5", 5), ("s3", 7), ("s6", 3),
        ("s4", 6), ("og", 4), ("s5", 6), ("s6", 4), ("s4", 7), ("s5", 7), ("s6", 5), ("grad", 0), ("grad", 1),
        ("grad", 2), ("grad", 3), ("s6", 6), ("s6", 7), ("s7",),
    )


def kernel(
    tokens, gate_w, up_w, down_w, out_grad, mixed, down_grad,
    w, wd, tok, og, part, core_in, y_out, y_in, hid, hid_t, x_own, x_out, x_in, z_out, z_in,
    w_sem, *sem_refs,
):
    ff = gate_w.shape[1]
    row, col = lax.axis_index("row"), lax.axis_index("col")
    y, c, x, z = row // 2, row % 2, col // NZ, col % NZ

    def dev(px, py, pz, pc):
        return (py * 2 + pc, px * NZ + pz)

    x_peer = [dev((x + j) % NX, y, z, c) for j in range(NX)]
    y_peer = [dev(x, (y + j) % NY, z, c) for j in range(NY)]
    z_peer = [dev(x, y, (z + j) % NZ, c) for j in range(NZ)]
    z_up, z_down = z_peer[1], z_peer[NZ - 1]
    sibling = dev(x, y, z, 1 - c)

    sems = {name: sem_refs[2 * i:2 * i + 2] for i, name in enumerate(SEMS)}
    started, seen = {}, set()

    def copy(key, src, dst, to):
        (ss, rs), at = sems[key[0]], key[1:]
        return pltpu.make_async_remote_copy(
            src_ref=src, dst_ref=dst, send_sem=ss.at[at], recv_sem=rs.at[at], device_id=to, device_id_type=MESH)

    def send(key, src, dst, to):
        copy(key, src, dst, to).start()
        started[key] = (src, dst)

    def arrived(*key):
        dst = started[key][1]
        copy(key, dst, dst, sibling).wait_recv()
        seen.add(key)

    loads = [
        pltpu.make_async_copy(tokens, tok.at[0, x], w_sem.at[3]),
        pltpu.make_async_copy(out_grad, og.at[0, x], w_sem.at[4]),
        pltpu.make_async_copy(gate_w, w.at[:, pl.ds(0, ff)], w_sem.at[0]),
        pltpu.make_async_copy(up_w, w.at[:, pl.ds(ff, ff)], w_sem.at[1]),
        pltpu.make_async_copy(down_w, wd, w_sem.at[2]),
    ]
    for load in loads:
        load.start()

    barrier = pltpu.get_barrier_semaphore()
    peers = x_peer[1:] + y_peer[1:] + z_peer[1:] + [sibling]
    for peer in peers:
        pl.semaphore_signal(barrier, inc=1, device_id=peer, device_id_type=MESH)
    loads[0].wait()
    loads[1].wait()
    pl.semaphore_wait(barrier, len(peers))

    def op_tokr(r):
        if r == 0:
            for q in FAR_FIRST:
                send(("zt", q), tok.at[0, x], tok.at[q, x], z_peer[NZ - q])
        else:
            arrived("zt", r)
        for j in (2, 1, 3):
            send(("xt", r, j - 1), tok.at[r, x], tok.at[r, x], x_peer[j])

    def ring(name, buf, rows, r):
        full, last = NZ // 2 - 1, NZ // 2
        lo, hi = pl.ds(0, rows // 2), pl.ds(rows // 2, rows // 2)
        if r < full:
            send((name, r + 1), buf(r), buf(r + 1), z_down)
        if r == full:
            send((name, 0), buf(r, hi), buf(last, hi), z_down)
        if r == last + 1:
            send((name, last), buf(r, lo), buf(last, lo), z_up)
        if r == 0 or r > last + 1:
            send((name, (r - 1) % NZ), buf(r), buf((r - 1) % NZ), z_up)

    def og_at(r, blocks=None):
        return og.at[r] if blocks is None else og.at[r, blocks]

    def ring_arrived(name, r):
        arrived(name, r)
        if r == NZ // 2:
            arrived(name, 0)

    def op_og_start():
        for j in (2, 1, 3):
            send(("ox", j - 1), og.at[0, x], og.at[0, x], x_peer[j])

    def op_og(d):
        if d == 0:
            for j in range(1, NX):
                arrived("ox", j - 1)
        for r in {0: (0,), NZ // 2: (NZ // 2,)}.get(d, (d, NZ - d)):
            if d > 0:
                ring_arrived("oz", r)
            ring("oz", og_at, NX, r)

    def op_s1(p):
        r = ORDER[p]
        if p == 0:
            loads[2].wait()
            loads[3].wait()
        for j in range(1, NX):
            arrived("xt", r, j - 1)
        a = tok[r].reshape(CHUNK, tokens.shape[1])

        for n in range(w.shape[1] // 256):
            cols = pl.ds(n * 256, 256)
            part[r, :, :, :, cols] = jnp.dot(a, w[:, cols], preferred_element_type=F32).reshape(2, NY, PART, 256)

        send(("c1", r), part.at[r, 1 - c], core_in.at[r], sibling)

    def op_s2(p):
        r = ORDER[p]
        arrived("c1", r)
        for j in (2, 1, 3):
            to = (y + j) % NY
            y_out[r, j - 1] = (part[r, c, to] + core_in[r, to]).astype(BF16)
            send(("y1", r, j - 1), y_out.at[r, j - 1], y_in.at[r, j - 1], y_peer[j])

    def op_s3(p):
        r = ORDER[p]
        total = part[r, c, y] + core_in[r, y]
        for j in (1, 3, 2):
            arrived("y1", r, j - 1)
            total = total + y_in[r, j - 1].astype(F32)
        gate, up = total[:, :ff], total[:, ff:]
        hid[r, c * NY + y] = (gate / (1.0 + jnp.exp(-gate)) * up).astype(BF16)
        mine = hid.at[r, c * NY + y]
        for j in (2, 1, 3):
            send(("y2", r, j - 1), mine, mine, y_peer[j])

    def op_s4(p):
        r = ORDER[p]
        for j in (1, 3, 2):
            arrived("y2", r, j - 1)
        mine = hid.at[r, pl.ds(c * NY, NY)]
        send(("c2", r), mine, mine, sibling)

    def op_s5(p):
        r = ORDER[p]
        if p == 0:
            loads[4].wait()
        arrived("c2", r)
        h = hid[r].reshape(CHUNK, ff)

        for n in range(wd.shape[1] // 256):
            cols = pl.ds(n * 256, 256)
            out = jnp.dot(h, wd[:, cols], preferred_element_type=F32).reshape(NX, OWN, 256)
            x_own[r, :, :, cols] = out
            x_out[r, :, :, cols] = out.astype(BF16)

        for j in (2, 1, 3):
            send(("x2", r, j - 1), x_out.at[r, (x + j) % NX], x_in.at[r, j - 1], x_peer[j])
        hid_t[:, pl.ds(r * CHUNK, CHUNK)] = h.T

    def op_s6(p):
        r = ORDER[p]
        total = x_own[r, x]
        for j in (1, 3, 2):
            arrived("x2", r, j - 1)
            total = total + x_in[r, j - 1].astype(F32)
        if r == 0:
            x_own[0, x] = total
        else:
            z_out[r] = total.astype(BF16)
            send(("z2", r), z_out.at[r], z_in.at[r], z_peer[r])

    def op_grad(n):
        cols = pl.ds(n * 256, 256)
        down_grad[:, cols] = jnp.dot(
            hid_t[...], og[:, :, :, cols].reshape(NZ * CHUNK, 256), preferred_element_type=F32)

    def op_s7():
        total = x_own[0, x]
        for r in ORDER[1:]:
            arrived("z2", r)
            total = total + z_in[r].astype(F32)
        mixed[...] = total.astype(BF16)

    ops = {"tokr": op_tokr, "og_start": op_og_start, "og": op_og, "s1": op_s1, "s2": op_s2, "s3": op_s3, "s4": op_s4,
           "s5": op_s5, "s6": op_s6, "grad": op_grad, "s7": op_s7}
    for op in schedule()[:CUT]:
        ops[op[0]](*op[1:])
    if CUT is not None:
        for key in started:
            if key not in seen:
                arrived(*key)
        done = {op for op in schedule()[:CUT]}
        if ("s1", 0) not in done:
            loads[2].wait()
            loads[3].wait()
        if ("s5", 0) not in done:
            loads[4].wait()
    for key, (src, _) in started.items():
        copy(key, src, src, sibling).wait_send()


def finish(mixed, down_grad, mixed_out, down_grad_out, sem):
    copies = [
        pltpu.make_async_copy(mixed, mixed_out, sem.at[0]),
        pltpu.make_async_copy(down_grad, down_grad_out, sem.at[1]),
    ]
    for copy in copies:
        copy.start()
    for copy in copies:
        copy.wait()


SEMS = {
    "zt": (NZ,), "xt": (NZ, NX - 1), "c1": (NZ,), "y1": (NZ, NY - 1), "y2": (NZ, NY - 1),
    "c2": (NZ,), "x2": (NZ, NX - 1), "z2": (NZ,), "ox": (NX - 1,), "oz": (NZ,),
}


def local(tokens, gate_w, up_w, down_w, out_grad):
    d, ff = gate_w.shape
    dma = pltpu.SemaphoreType.DMA
    vmem, hbm = pl.BlockSpec(memory_space=pltpu.VMEM), pl.BlockSpec(memory_space=pltpu.HBM)
    mixed, down_grad = pl.pallas_call(
        kernel,
        out_shape=(
            pltpu.VMEM((OWN, d), BF16),
            pltpu.VMEM((ff, d), F32),
        ),
        in_specs=[hbm] * 5,
        out_specs=(vmem, vmem),
        scratch_shapes=[
            pltpu.VMEM((d, 2 * ff), BF16),
            pltpu.VMEM((ff, d), BF16),
            pltpu.VMEM((NZ, NX, OWN, d), BF16),
            pltpu.VMEM((NZ, NX, OWN, d), BF16),
            pltpu.VMEM((NZ, 2, NY, PART, 2 * ff), F32),
            pltpu.VMEM((NZ, NY, PART, 2 * ff), F32),
            pltpu.VMEM((NZ, NY - 1, PART, 2 * ff), BF16),
            pltpu.VMEM((NZ, NY - 1, PART, 2 * ff), BF16),
            pltpu.VMEM((NZ, 2 * NY, PART, ff), BF16),
            pltpu.VMEM((ff, NZ * CHUNK), BF16),
            pltpu.VMEM((NZ, NX, OWN, d), F32),
            pltpu.VMEM((NZ, NX, OWN, d), BF16),
            pltpu.VMEM((NZ, NX - 1, OWN, d), BF16),
            pltpu.VMEM((NZ, OWN, d), BF16),
            pltpu.VMEM((NZ, OWN, d), BF16),
            dma((5,)),
            *[dma(shape) for shape in SEMS.values() for _ in range(2)],
        ],
        compiler_params=pltpu.CompilerParams(
            collective_id=0, has_side_effects=True, vmem_limit_bytes=42 * 2**20),
        cost_estimate=pl.CostEstimate(flops=7_600_000_000, bytes_accessed=10_000_000, transcendentals=120_000),
    )(*[pltpu.with_memory_space_constraint(a, pltpu.HBM) for a in (tokens, gate_w, up_w, down_w, out_grad)])
    return pl.pallas_call(
        finish,
        out_shape=(
            jax.ShapeDtypeStruct((OWN, d), BF16),
            jax.ShapeDtypeStruct((ff, d), F32),
        ),
        in_specs=[vmem, vmem],
        out_specs=(hbm, hbm),
        scratch_shapes=[dma((2,))],
        compiler_params=pltpu.CompilerParams(vmem_limit_bytes=2**20),
    )(*[pltpu.with_memory_space_constraint(a, pltpu.VMEM) for a in (mixed, down_grad)])


def solution(mesh):
    return jax.shard_map(
        local,
        mesh=mesh,
        in_specs=(P("col", "row"), P("row", "col"), P("row", "col"), P("col", "row"), P("col", "row")),
        out_specs=(P("col", "row"), P("col", "row")),
        check_vma=False,
    )
```

```python
import jax
import jax.numpy as jnp
from jax import lax
from jax.experimental import pallas as pl
from jax.experimental.pallas import tpu as pltpu
from jax.sharding import PartitionSpec as P

MESH = pl.DeviceIdType.MESH
BF16, F32 = jnp.bfloat16, jnp.float32
NX, NY, NZ = 4, 4, 8
OWN = 32
CHUNK = NX * OWN
PART = CHUNK // (2 * NY)


ORDER = (0, 7, 2, 3, 1, 4, 5, 6)

def schedule():
    return (
        ("tokr", 0), ("zs", 2), ("zs", 7), ("zs", 5), ("og_start",), ("tokr", 7), ("zs", 4), ("s1", 0), ("zs", 3),
        ("ogs", 0), ("tokr", 2), ("tokr", 5), ("zs", 6), ("s2", 0), ("s1", 1), ("s2", 1), ("s1", 2), ("tokr", 4),
        ("zs", 1), ("s3", 0), ("s2", 2), ("ogs", 7), ("s1", 6), ("tokr", 3), ("s2", 6), ("s3", 1), ("tokr", 6),
        ("ogs", 1), ("s4", 0), ("s1", 5), ("s5", 0), ("s3", 2), ("tokr", 1), ("s2", 5), ("ogs", 6), ("s1", 3),
        ("s4", 1), ("s3", 6), ("s1", 7), ("s2", 3), ("s5", 1), ("ogs", 2), ("s4", 2), ("s3", 5), ("s5", 2),
        ("s2", 7), ("s1", 4), ("s3", 3), ("s4", 6), ("s2", 4), ("s5", 6), ("s4", 5), ("s3", 7), ("s5", 5),
        ("ogs", 3), ("s4", 3), ("ogs", 5), ("s6", 2), ("s5", 3), ("s3", 4), ("s4", 7), ("s6", 6), ("s5", 7),
        ("s4", 4), ("s6", 5), ("ogs", 4), ("s6", 0), ("s6", 1), ("s5", 4), ("s6", 3), ("s6", 7), ("grad", 3),
        ("s6", 4), ("grad", 1), ("grad", 2), ("grad", 0), ("s7",),
    )


def kernel(
    tokens, gate_w, up_w, down_w, out_grad, mixed, down_grad,
    w, wd, tok, og, part, core_in, y_out, y_in, hid, hid_t, x_own, x_out, x_in, z_out, z_in,
    w_sem, *sem_refs,
):
    ff = gate_w.shape[1]
    row, col = lax.axis_index("row"), lax.axis_index("col")
    y, c, x, z = row // 2, row % 2, col // NZ, col % NZ

    def dev(px, py, pz, pc):
        return (py * 2 + pc, px * NZ + pz)

    x_peer = [dev((x + j) % NX, y, z, c) for j in range(NX)]
    y_peer = [dev(x, (y + j) % NY, z, c) for j in range(NY)]
    z_peer = [dev(x, y, (z + j) % NZ, c) for j in range(NZ)]
    z_up, z_down = z_peer[1], z_peer[NZ - 1]
    sibling = dev(x, y, z, 1 - c)

    sems = {name: sem_refs[2 * i:2 * i + 2] for i, name in enumerate(SEMS)}
    started = {}

    def copy(key, src, dst, to):
        (ss, rs), at = sems[key[0]], key[1:]
        return pltpu.make_async_remote_copy(
            src_ref=src, dst_ref=dst, send_sem=ss.at[at], recv_sem=rs.at[at], device_id=to, device_id_type=MESH)

    def send(key, src, dst, to):
        copy(key, src, dst, to).start()
        started[key] = (src, dst)

    def arrived(*key):
        dst = started[key][1]
        copy(key, dst, dst, sibling).wait_recv()

    loads = [
        pltpu.make_async_copy(tokens, tok.at[0, x], w_sem.at[3]),
        pltpu.make_async_copy(out_grad, og.at[0, x], w_sem.at[4]),
        pltpu.make_async_copy(gate_w, w.at[:, pl.ds(0, ff)], w_sem.at[0]),
        pltpu.make_async_copy(up_w, w.at[:, pl.ds(ff, ff)], w_sem.at[1]),
        pltpu.make_async_copy(down_w, wd, w_sem.at[2]),
    ]
    for load in loads:
        load.start()

    barrier = pltpu.get_barrier_semaphore()
    peers = x_peer[1:] + y_peer[1:] + z_peer[1:] + [sibling]
    for peer in peers:
        pl.semaphore_signal(barrier, inc=1, device_id=peer, device_id_type=MESH)
    loads[0].wait()
    loads[1].wait()
    pl.semaphore_wait(barrier, len(peers))

    def op_zs(r):
        send(("zt", r), tok.at[0, x], tok.at[r, x], z_peer[NZ - r])

    def op_tokr(r):
        if r > 0:
            arrived("zt", r)
        for j in (2, 1, 3):
            send(("xt", r, j - 1), tok.at[r, x], tok.at[r, x], x_peer[j])

    def ring(name, buf, rows, r):
        full, last = NZ // 2 - 1, NZ // 2
        lo, hi = pl.ds(0, rows // 2), pl.ds(rows // 2, rows // 2)
        if r < full:
            send((name, r + 1), buf(r), buf(r + 1), z_down)
        if r == full:
            send((name, 0), buf(r, hi), buf(last, hi), z_down)
        if r == last + 1:
            send((name, last), buf(r, lo), buf(last, lo), z_up)
        if r == 0 or r > last + 1:
            send((name, (r - 1) % NZ), buf(r), buf((r - 1) % NZ), z_up)

    def og_at(r, blocks=None):
        return og.at[r] if blocks is None else og.at[r, blocks]

    def ring_arrived(name, r):
        arrived(name, r)
        if r == NZ // 2:
            arrived(name, 0)

    def op_og_start():
        for j in (2, 1, 3):
            send(("ox", j - 1), og.at[0, x], og.at[0, x], x_peer[j])

    def op_ogs(r):
        if r == 0:
            for j in range(1, NX):
                arrived("ox", j - 1)
        else:
            ring_arrived("oz", r)
        ring("oz", og_at, NX, r)

    def op_s1(p):
        r = ORDER[p]
        if p == 0:
            loads[2].wait()
            loads[3].wait()
        for j in range(1, NX):
            arrived("xt", r, j - 1)
        a = tok[r].reshape(CHUNK, tokens.shape[1])

        for n in range(w.shape[1] // 256):
            cols = pl.ds(n * 256, 256)
            part[r, :, :, :, cols] = jnp.dot(a, w[:, cols], preferred_element_type=F32).reshape(2, NY, PART, 256)

        send(("c1", r), part.at[r, 1 - c], core_in.at[r], sibling)

    def op_s2(p):
        r = ORDER[p]
        arrived("c1", r)
        for j in (2, 1, 3):
            to = (y + j) % NY
            y_out[r, j - 1] = (part[r, c, to] + core_in[r, to]).astype(BF16)
            send(("y1", r, j - 1), y_out.at[r, j - 1], y_in.at[r, j - 1], y_peer[j])

    def op_s3(p):
        r = ORDER[p]
        total = part[r, c, y] + core_in[r, y]
        for j in (1, 3, 2):
            arrived("y1", r, j - 1)
            total = total + y_in[r, j - 1].astype(F32)
        gate, up = total[:, :ff], total[:, ff:]
        hid[r, c * NY + y] = (gate / (1.0 + jnp.exp(-gate)) * up).astype(BF16)
        mine = hid.at[r, c * NY + y]
        for j in (2, 1, 3):
            send(("y2", r, j - 1), mine, mine, y_peer[j])

    def op_s4(p):
        r = ORDER[p]
        for j in (1, 3, 2):
            arrived("y2", r, j - 1)
        mine = hid.at[r, pl.ds(c * NY, NY)]
        send(("c2", r), mine, mine, sibling)

    def op_s5(p):
        r = ORDER[p]
        if p == 0:
            loads[4].wait()
        arrived("c2", r)
        h = hid[r].reshape(CHUNK, ff)

        for n in range(wd.shape[1] // 256):
            cols = pl.ds(n * 256, 256)
            out = jnp.dot(h, wd[:, cols], preferred_element_type=F32).reshape(NX, OWN, 256)
            x_own[r, :, :, cols] = out
            x_out[r, :, :, cols] = out.astype(BF16)

        for j in (2, 1, 3):
            send(("x2", r, j - 1), x_out.at[r, (x + j) % NX], x_in.at[r, j - 1], x_peer[j])
        hid_t[:, pl.ds(r * CHUNK, CHUNK)] = h.T

    def op_s6(p):
        r = ORDER[p]
        total = x_own[r, x]
        for j in (1, 3, 2):
            arrived("x2", r, j - 1)
            total = total + x_in[r, j - 1].astype(F32)
        if r == 0:
            x_own[0, x] = total
        else:
            z_out[r] = total.astype(BF16)
            send(("z2", r), z_out.at[r], z_in.at[r], z_peer[r])

    def op_grad(n):
        cols = pl.ds(n * 256, 256)
        down_grad[:, cols] = jnp.dot(
            hid_t[...], og[:, :, :, cols].reshape(NZ * CHUNK, 256), preferred_element_type=F32)

    def op_s7():
        total = x_own[0, x]
        for r in ORDER[1:]:
            arrived("z2", r)
            total = total + z_in[r].astype(F32)
        mixed[...] = total.astype(BF16)

    ops = {"zs": op_zs, "tokr": op_tokr, "og_start": op_og_start, "ogs": op_ogs, "s1": op_s1, "s2": op_s2, "s3": op_s3, "s4": op_s4,
           "s5": op_s5, "s6": op_s6, "grad": op_grad, "s7": op_s7}
    for op in schedule():
        ops[op[0]](*op[1:])
    for key, (src, _) in started.items():
        copy(key, src, src, sibling).wait_send()


def finish(mixed, down_grad, mixed_out, down_grad_out, sem):
    copies = [
        pltpu.make_async_copy(mixed, mixed_out, sem.at[0]),
        pltpu.make_async_copy(down_grad, down_grad_out, sem.at[1]),
    ]
    for copy in copies:
        copy.start()
    for copy in copies:
        copy.wait()


SEMS = {
    "zt": (NZ,), "xt": (NZ, NX - 1), "c1": (NZ,), "y1": (NZ, NY - 1), "y2": (NZ, NY - 1),
    "c2": (NZ,), "x2": (NZ, NX - 1), "z2": (NZ,), "ox": (NX - 1,), "oz": (NZ,),
}


def local(tokens, gate_w, up_w, down_w, out_grad):
    d, ff = gate_w.shape
    dma = pltpu.SemaphoreType.DMA
    vmem, hbm = pl.BlockSpec(memory_space=pltpu.VMEM), pl.BlockSpec(memory_space=pltpu.HBM)
    mixed, down_grad = pl.pallas_call(
        kernel,
        out_shape=(
            pltpu.VMEM((OWN, d), BF16),
            pltpu.VMEM((ff, d), F32),
        ),
        in_specs=[hbm] * 5,
        out_specs=(vmem, vmem),
        scratch_shapes=[
            pltpu.VMEM((d, 2 * ff), BF16),
            pltpu.VMEM((ff, d), BF16),
            pltpu.VMEM((NZ, NX, OWN, d), BF16),
            pltpu.VMEM((NZ, NX, OWN, d), BF16),
            pltpu.VMEM((NZ, 2, NY, PART, 2 * ff), F32),
            pltpu.VMEM((NZ, NY, PART, 2 * ff), F32),
            pltpu.VMEM((NZ, NY - 1, PART, 2 * ff), BF16),
            pltpu.VMEM((NZ, NY - 1, PART, 2 * ff), BF16),
            pltpu.VMEM((NZ, 2 * NY, PART, ff), BF16),
            pltpu.VMEM((ff, NZ * CHUNK), BF16),
            pltpu.VMEM((NZ, NX, OWN, d), F32),
            pltpu.VMEM((NZ, NX, OWN, d), BF16),
            pltpu.VMEM((NZ, NX - 1, OWN, d), BF16),
            pltpu.VMEM((NZ, OWN, d), BF16),
            pltpu.VMEM((NZ, OWN, d), BF16),
            dma((5,)),
            *[dma(shape) for shape in SEMS.values() for _ in range(2)],
        ],
        compiler_params=pltpu.CompilerParams(
            collective_id=0, has_side_effects=True, vmem_limit_bytes=42 * 2**20),
        cost_estimate=pl.CostEstimate(flops=7_600_000_000, bytes_accessed=10_000_000, transcendentals=120_000),
    )(*[pltpu.with_memory_space_constraint(a, pltpu.HBM) for a in (tokens, gate_w, up_w, down_w, out_grad)])
    return pl.pallas_call(
        finish,
        out_shape=(
            jax.ShapeDtypeStruct((OWN, d), BF16),
            jax.ShapeDtypeStruct((ff, d), F32),
        ),
        in_specs=[vmem, vmem],
        out_specs=(hbm, hbm),
        scratch_shapes=[dma((2,))],
        compiler_params=pltpu.CompilerParams(vmem_limit_bytes=2**20),
    )(*[pltpu.with_memory_space_constraint(a, pltpu.VMEM) for a in (mixed, down_grad)])


def solution(mesh):
    return jax.shard_map(
        local,
        mesh=mesh,
        in_specs=(P("col", "row"), P("row", "col"), P("row", "col"), P("col", "row"), P("col", "row")),
        out_specs=(P("col", "row"), P("col", "row")),
        check_vma=False,
    )
```

```python
import jax
import jax.numpy as jnp
from jax import lax
from jax.experimental import pallas as pl
from jax.experimental.pallas import tpu as pltpu
from jax.sharding import PartitionSpec as P

MESH = pl.DeviceIdType.MESH
BF16, F32 = jnp.bfloat16, jnp.float32
NX, NY, NZ = 4, 4, 8
OWN = 32
CHUNK = NX * OWN
PART = CHUNK // (2 * NY)


ORDER = (0, 7, 2, 3, 1, 4, 5, 6)


def schedule():
    return (
        ("tokr", 0), ("zs", 2), ("zs", 7), ("zs", 5), ("og_start",), ("tokr", 7), ("zs", 4), ("s1", 0), ("zs", 3),
        ("ogs", 0), ("tokr", 2), ("tokr", 5), ("zs", 6), ("s2", 0), ("s1", 1), ("s2", 1), ("s1", 2), ("tokr", 4),
        ("zs", 1), ("s3", 0), ("s2", 2), ("ogs", 7), ("s1", 6), ("tokr", 3), ("s2", 6), ("s3", 1), ("tokr", 6),
        ("ogs", 1), ("s4", 0), ("s1", 5), ("s5", 0), ("s3", 2), ("tokr", 1), ("s2", 5), ("ogs", 6), ("s1", 3),
        ("s4", 1), ("s3", 6), ("s1", 7), ("s2", 3), ("s5", 1), ("ogs", 2), ("s4", 2), ("s3", 5), ("s5", 2),
        ("s2", 7), ("s1", 4), ("s3", 3), ("s4", 6), ("s2", 4), ("s5", 6), ("s4", 5), ("s3", 7), ("s5", 5),
        ("ogs", 3), ("s4", 3), ("ogs", 5), ("s6", 2), ("s5", 3), ("s3", 4), ("s4", 7), ("s6", 6), ("s5", 7),
        ("s4", 4), ("s6", 5), ("ogs", 4), ("s6", 0), ("s6", 1), ("s5", 4), ("s6", 3), ("s6", 7), ("grad", 3),
        ("s6", 4), ("grad", 1), ("grad", 2), ("grad", 0), ("s7",),
    )


def kernel(
    tokens, gate_w, up_w, down_w, out_grad, mixed, down_grad,
    w, wd, tok, og, part, core_in, y_out, y_in, hid, hid_t, x_own, x_out, x_in, z_out, z_in,
    w_sem, *sem_refs,
):
    ff = gate_w.shape[1]
    row, col = lax.axis_index("row"), lax.axis_index("col")
    y, c, x, z = row // 2, row % 2, col // NZ, col % NZ

    def dev(px, py, pz, pc):
        return (py * 2 + pc, px * NZ + pz)

    x_peer = [dev((x + j) % NX, y, z, c) for j in range(NX)]
    y_peer = [dev(x, (y + j) % NY, z, c) for j in range(NY)]
    z_peer = [dev(x, y, (z + j) % NZ, c) for j in range(NZ)]
    z_up, z_down = z_peer[1], z_peer[NZ - 1]
    sibling = dev(x, y, z, 1 - c)

    sems = {name: sem_refs[2 * i:2 * i + 2] for i, name in enumerate(SEMS)}
    started = {}

    def copy(key, src, dst, to):
        (ss, rs), at = sems[key[0]], key[1:]
        return pltpu.make_async_remote_copy(
            src_ref=src, dst_ref=dst, send_sem=ss.at[at], recv_sem=rs.at[at], device_id=to, device_id_type=MESH)

    def send(key, src, dst, to):
        copy(key, src, dst, to).start()
        started[key] = (src, dst)

    def arrived(*key):
        dst = started[key][1]
        copy(key, dst, dst, sibling).wait_recv()

    loads = [
        pltpu.make_async_copy(tokens, tok.at[0, x], w_sem.at[3]),
        pltpu.make_async_copy(out_grad, og.at[0, x], w_sem.at[4]),
        pltpu.make_async_copy(gate_w, w.at[:, pl.ds(0, ff)], w_sem.at[0]),
        pltpu.make_async_copy(up_w, w.at[:, pl.ds(ff, ff)], w_sem.at[1]),
        pltpu.make_async_copy(down_w, wd, w_sem.at[2]),
    ]
    for load in loads:
        load.start()

    barrier = pltpu.get_barrier_semaphore()
    peers = x_peer[1:] + y_peer[1:] + z_peer[1:] + [sibling]
    for peer in peers:
        pl.semaphore_signal(barrier, inc=1, device_id=peer, device_id_type=MESH)
    loads[0].wait()
    loads[1].wait()
    pl.semaphore_wait(barrier, len(peers))

    def op_zs(r):
        send(("zt", r), tok.at[0, x], tok.at[r, x], z_peer[NZ - r])

    def op_tokr(r):
        if r > 0:
            arrived("zt", r)
        for j in (2, 1, 3):
            send(("xt", r, j - 1), tok.at[r, x], tok.at[r, x], x_peer[j])

    def ring(name, buf, rows, r):
        full, last = NZ // 2 - 1, NZ // 2
        lo, hi = pl.ds(0, rows // 2), pl.ds(rows // 2, rows // 2)
        if r < full:
            send((name, r + 1), buf(r), buf(r + 1), z_down)
        if r == full:
            send((name, 0), buf(r, hi), buf(last, hi), z_down)
        if r == last + 1:
            send((name, last), buf(r, lo), buf(last, lo), z_up)
        if r == 0 or r > last + 1:
            send((name, (r - 1) % NZ), buf(r), buf((r - 1) % NZ), z_up)

    def og_at(r, blocks=None):
        return og.at[r] if blocks is None else og.at[r, blocks]

    def ring_arrived(name, r):
        arrived(name, r)
        if r == NZ // 2:
            arrived(name, 0)

    def op_og_start():
        for j in (2, 1, 3):
            send(("ox", j - 1), og.at[0, x], og.at[0, x], x_peer[j])

    def op_ogs(r):
        if r == 0:
            for j in range(1, NX):
                arrived("ox", j - 1)
        else:
            ring_arrived("oz", r)
        ring("oz", og_at, NX, r)

    def op_s1(p):
        r = ORDER[p]
        if p == 0:
            loads[2].wait()
            loads[3].wait()
        for j in range(1, NX):
            arrived("xt", r, j - 1)
        a = tok[r].reshape(CHUNK, tokens.shape[1])

        for n in range(w.shape[1] // 256):
            cols = pl.ds(n * 256, 256)
            part[r, :, :, :, cols] = jnp.dot(a, w[:, cols], preferred_element_type=F32).reshape(2, NY, PART, 256)

        send(("c1", r), part.at[r, 1 - c], core_in.at[r], sibling)

    def op_s2(p):
        r = ORDER[p]
        arrived("c1", r)
        for j in (2, 1, 3):
            to = (y + j) % NY
            y_out[r, j - 1] = (part[r, c, to] + core_in[r, to]).astype(BF16)
            send(("y1", r, j - 1), y_out.at[r, j - 1], y_in.at[r, j - 1], y_peer[j])

    def op_s3(p):
        r = ORDER[p]
        total = part[r, c, y] + core_in[r, y]
        for j in (1, 3, 2):
            arrived("y1", r, j - 1)
            total = total + y_in[r, j - 1].astype(F32)
        gate, up = total[:, :ff], total[:, ff:]
        hid[r, c * NY + y] = (gate / (1.0 + jnp.exp(-gate)) * up).astype(BF16)
        mine = hid.at[r, c * NY + y]
        for j in (2, 1, 3):
            send(("y2", r, j - 1), mine, mine, y_peer[j])

    def op_s4(p):
        r = ORDER[p]
        for j in (1, 3, 2):
            arrived("y2", r, j - 1)
        mine = hid.at[r, pl.ds(c * NY, NY)]
        send(("c2", r), mine, mine, sibling)

    def op_s5(p):
        r = ORDER[p]
        if p == 0:
            loads[4].wait()
        arrived("c2", r)
        h = hid[r].reshape(CHUNK, ff)

        for n in range(wd.shape[1] // 256):
            cols = pl.ds(n * 256, 256)
            out = jnp.dot(h, wd[:, cols], preferred_element_type=F32).reshape(NX, OWN, 256)
            x_own[r, :, :, cols] = out
            x_out[r, :, :, cols] = out.astype(BF16)

        for j in (2, 1, 3):
            send(("x2", r, j - 1), x_out.at[r, (x + j) % NX], x_in.at[r, j - 1], x_peer[j])
        hid_t[:, pl.ds(r * CHUNK, CHUNK)] = h.T

    def op_s6(p):
        r = ORDER[p]
        total = x_own[r, x]
        for j in (1, 3, 2):
            arrived("x2", r, j - 1)
            total = total + x_in[r, j - 1].astype(F32)
        if r == 0:
            x_own[0, x] = total
        else:
            z_out[r] = total.astype(BF16)
            send(("z2", r), z_out.at[r], z_in.at[r], z_peer[r])

    def op_grad(n):
        cols = pl.ds(n * 256, 256)
        down_grad[:, cols] = jnp.dot(
            hid_t[...], og[:, :, :, cols].reshape(NZ * CHUNK, 256), preferred_element_type=F32)

    def op_s7():
        for key, (src, _) in started.items():
            copy(key, src, src, sibling).wait_send()
        total = x_own[0, x]
        for r in ORDER[1:]:
            arrived("z2", r)
            total = total + z_in[r].astype(F32)
        mixed[...] = total.astype(BF16)

    ops = {"zs": op_zs, "tokr": op_tokr, "og_start": op_og_start, "ogs": op_ogs, "s1": op_s1, "s2": op_s2, "s3": op_s3, "s4": op_s4,
           "s5": op_s5, "s6": op_s6, "grad": op_grad, "s7": op_s7}
    for op in schedule():
        ops[op[0]](*op[1:])


def finish(mixed, down_grad, mixed_out, down_grad_out, sem):
    copies = [
        pltpu.make_async_copy(mixed, mixed_out, sem.at[0]),
        pltpu.make_async_copy(down_grad, down_grad_out, sem.at[1]),
    ]
    for copy in copies:
        copy.start()
    for copy in copies:
        copy.wait()


SEMS = {
    "zt": (NZ,), "xt": (NZ, NX - 1), "c1": (NZ,), "y1": (NZ, NY - 1), "y2": (NZ, NY - 1),
    "c2": (NZ,), "x2": (NZ, NX - 1), "z2": (NZ,), "ox": (NX - 1,), "oz": (NZ,),
}


def local(tokens, gate_w, up_w, down_w, out_grad):
    d, ff = gate_w.shape
    dma = pltpu.SemaphoreType.DMA
    vmem, hbm = pl.BlockSpec(memory_space=pltpu.VMEM), pl.BlockSpec(memory_space=pltpu.HBM)
    mixed, down_grad = pl.pallas_call(
        kernel,
        out_shape=(
            pltpu.VMEM((OWN, d), BF16),
            pltpu.VMEM((ff, d), F32),
        ),
        in_specs=[hbm] * 5,
        out_specs=(vmem, vmem),
        scratch_shapes=[
            pltpu.VMEM((d, 2 * ff), BF16),
            pltpu.VMEM((ff, d), BF16),
            pltpu.VMEM((NZ, NX, OWN, d), BF16),
            pltpu.VMEM((NZ, NX, OWN, d), BF16),
            pltpu.VMEM((NZ, 2, NY, PART, 2 * ff), F32),
            pltpu.VMEM((NZ, NY, PART, 2 * ff), F32),
            pltpu.VMEM((NZ, NY - 1, PART, 2 * ff), BF16),
            pltpu.VMEM((NZ, NY - 1, PART, 2 * ff), BF16),
            pltpu.VMEM((NZ, 2 * NY, PART, ff), BF16),
            pltpu.VMEM((ff, NZ * CHUNK), BF16),
            pltpu.VMEM((NZ, NX, OWN, d), F32),
            pltpu.VMEM((NZ, NX, OWN, d), BF16),
            pltpu.VMEM((NZ, NX - 1, OWN, d), BF16),
            pltpu.VMEM((NZ, OWN, d), BF16),
            pltpu.VMEM((NZ, OWN, d), BF16),
            dma((5,)),
            *[dma(shape) for shape in SEMS.values() for _ in range(2)],
        ],
        compiler_params=pltpu.CompilerParams(
            collective_id=0, has_side_effects=True, vmem_limit_bytes=42 * 2**20),
        cost_estimate=pl.CostEstimate(flops=7_600_000_000, bytes_accessed=10_000_000, transcendentals=120_000),
    )(*[pltpu.with_memory_space_constraint(a, pltpu.HBM) for a in (tokens, gate_w, up_w, down_w, out_grad)])
    return pl.pallas_call(
        finish,
        out_shape=(
            jax.ShapeDtypeStruct((OWN, d), BF16),
            jax.ShapeDtypeStruct((ff, d), F32),
        ),
        in_specs=[vmem, vmem],
        out_specs=(hbm, hbm),
        scratch_shapes=[dma((2,))],
        compiler_params=pltpu.CompilerParams(vmem_limit_bytes=2**20),
    )(*[pltpu.with_memory_space_constraint(a, pltpu.VMEM) for a in (mixed, down_grad)])


def solution(mesh):
    return jax.shard_map(
        local,
        mesh=mesh,
        in_specs=(P("col", "row"), P("row", "col"), P("row", "col"), P("col", "row"), P("col", "row")),
        out_specs=(P("col", "row"), P("col", "row")),
        check_vma=False,
    )
```

```python
import jax
import jax.numpy as jnp
from jax import lax
from jax.experimental import pallas as pl
from jax.experimental.pallas import tpu as pltpu
from jax.sharding import PartitionSpec as P

MESH = pl.DeviceIdType.MESH
BF16, F32 = jnp.bfloat16, jnp.float32
NX, NY, NZ = 4, 4, 8
OWN = 32
CHUNK = NX * OWN
PART = CHUNK // (2 * NY)


ORDER = (0, 7, 2, 3, 1, 4, 5, 6)


def schedule():
    return (
        ("tokr", 0), ("zs", 2), ("zs", 7), ("zs", 5), ("og_start",), ("tokr", 7), ("zs", 4), ("s1", 0), ("zs", 3),
        ("ogs", 0), ("tokr", 2), ("tokr", 5), ("zs", 6), ("s2", 0), ("s1", 1), ("s2", 1), ("s1", 2), ("tokr", 4),
        ("zs", 1), ("s3", 0), ("s2", 2), ("ogs", 7), ("s1", 6), ("tokr", 3), ("s2", 6), ("s3", 1), ("tokr", 6),
        ("ogs", 1), ("s4", 0), ("s1", 5), ("s5", 0), ("s3", 2), ("tokr", 1), ("s2", 5), ("ogs", 6), ("s1", 3),
        ("s4", 1), ("s3", 6), ("s1", 7), ("s2", 3), ("s5", 1), ("ogs", 2), ("s4", 2), ("s3", 5), ("s5", 2),
        ("s2", 7), ("s1", 4), ("s3", 3), ("s4", 6), ("s2", 4), ("s5", 6), ("s4", 5), ("s3", 7), ("s5", 5),
        ("ogs", 3), ("s4", 3), ("ogs", 5), ("s6", 2), ("s5", 3), ("s3", 4), ("s4", 7), ("s6", 6), ("s5", 7),
        ("s4", 4), ("s6", 5), ("ogs", 4), ("s6", 0), ("s6", 1), ("s5", 4), ("s6", 3), ("s6", 7), ("grad", 3),
        ("s6", 4), ("grad", 1), ("grad", 2), ("grad", 0), ("s7",),
    )


def kernel(
    tokens, gate_w, up_w, down_w, out_grad, mixed, down_grad,
    w, wd, tok, og, part, core_in, y_out, y_in, hid, hid_t, x_own, x_out, x_in, z_out, z_in,
    w_sem, *sem_refs,
):
    ff = gate_w.shape[1]
    row, col = lax.axis_index("row"), lax.axis_index("col")
    y, c, x, z = row // 2, row % 2, col // NZ, col % NZ

    def dev(px, py, pz, pc):
        return (py * 2 + pc, px * NZ + pz)

    x_peer = [dev((x + j) % NX, y, z, c) for j in range(NX)]
    y_peer = [dev(x, (y + j) % NY, z, c) for j in range(NY)]
    z_peer = [dev(x, y, (z + j) % NZ, c) for j in range(NZ)]
    z_up, z_down = z_peer[1], z_peer[NZ - 1]
    sibling = dev(x, y, z, 1 - c)

    sems = {name: sem_refs[2 * i:2 * i + 2] for i, name in enumerate(SEMS)}
    started = {}

    def copy(key, src, dst, to):
        (ss, rs), at = sems[key[0]], key[1:]
        return pltpu.make_async_remote_copy(
            src_ref=src, dst_ref=dst, send_sem=ss.at[at], recv_sem=rs.at[at], device_id=to, device_id_type=MESH)

    def send(key, src, dst, to):
        copy(key, src, dst, to).start()
        started[key] = (src, dst)

    def arrived(*key):
        dst = started[key][1]
        copy(key, dst, dst, sibling).wait_recv()

    loads = [
        pltpu.make_async_copy(tokens, tok.at[0, x], w_sem.at[3]),
        pltpu.make_async_copy(out_grad, og.at[0, x], w_sem.at[4]),
        pltpu.make_async_copy(gate_w, w.at[:, pl.ds(0, ff)], w_sem.at[0]),
        pltpu.make_async_copy(up_w, w.at[:, pl.ds(ff, ff)], w_sem.at[1]),
        pltpu.make_async_copy(down_w, wd, w_sem.at[2]),
    ]
    for load in loads:
        load.start()

    barrier = pltpu.get_barrier_semaphore()
    peers = [z_peer[j] for j in (4, 3, 5, 2, 6)] + [x_peer[2], y_peer[2]]
    peers += [z_up, z_down, x_peer[1], x_peer[3], y_peer[1], y_peer[3], sibling]
    for peer in peers:
        pl.semaphore_signal(barrier, inc=1, device_id=peer, device_id_type=MESH)
    loads[0].wait()
    loads[1].wait()
    pl.semaphore_wait(barrier, len(peers))

    def op_zs(r):
        send(("zt", r), tok.at[0, x], tok.at[r, x], z_peer[NZ - r])

    def op_tokr(r):
        if r > 0:
            arrived("zt", r)
        for j in (2, 1, 3):
            send(("xt", r, j - 1), tok.at[r, x], tok.at[r, x], x_peer[j])

    def ring(name, buf, rows, r):
        full, last = NZ // 2 - 1, NZ // 2
        lo, hi = pl.ds(0, rows // 2), pl.ds(rows // 2, rows // 2)
        if r < full:
            send((name, r + 1), buf(r), buf(r + 1), z_down)
        if r == full:
            send((name, 0), buf(r, hi), buf(last, hi), z_down)
        if r == last + 1:
            send((name, last), buf(r, lo), buf(last, lo), z_up)
        if r == 0 or r > last + 1:
            send((name, (r - 1) % NZ), buf(r), buf((r - 1) % NZ), z_up)

    def og_at(r, blocks=None):
        return og.at[r] if blocks is None else og.at[r, blocks]

    def ring_arrived(name, r):
        arrived(name, r)
        if r == NZ // 2:
            arrived(name, 0)

    def op_og_start():
        for j in (2, 1, 3):
            send(("ox", j - 1), og.at[0, x], og.at[0, x], x_peer[j])

    def op_ogs(r):
        if r == 0:
            for j in range(1, NX):
                arrived("ox", j - 1)
        else:
            ring_arrived("oz", r)
        ring("oz", og_at, NX, r)

    def op_s1(p):
        r = ORDER[p]
        if p == 0:
            loads[2].wait()
            loads[3].wait()
        for j in range(1, NX):
            arrived("xt", r, j - 1)
        a = tok[r].reshape(CHUNK, tokens.shape[1])

        for n in range(w.shape[1] // 256):
            cols = pl.ds(n * 256, 256)
            part[r, :, :, :, cols] = jnp.dot(a, w[:, cols], preferred_element_type=F32).reshape(2, NY, PART, 256)
            if n == 3 or n == w.shape[1] // 256 - 1:
                go = pl.ds(0, 1024) if n == 3 else pl.ds(1024, w.shape[1] - 1024)
                send(("c1", r, n // 4), part.at[r, 1 - c, :, :, go], core_in.at[r, :, :, go], sibling)

    def op_s2(p):
        r = ORDER[p]
        arrived("c1", r, 0)
        arrived("c1", r, 1)
        for j in (2, 1, 3):
            to = (y + j) % NY
            y_out[r, j - 1] = (part[r, c, to] + core_in[r, to]).astype(BF16)
            send(("y1", r, j - 1), y_out.at[r, j - 1], y_in.at[r, j - 1], y_peer[j])

    def op_s3(p):
        r = ORDER[p]
        total = part[r, c, y] + core_in[r, y]
        for j in (1, 3, 2):
            arrived("y1", r, j - 1)
            total = total + y_in[r, j - 1].astype(F32)
        gate, up = total[:, :ff], total[:, ff:]
        hid[r, c * NY + y] = (gate / (1.0 + jnp.exp(-gate)) * up).astype(BF16)
        mine = hid.at[r, c * NY + y]
        for j in (2, 1, 3):
            send(("y2", r, j - 1), mine, mine, y_peer[j])

    def op_s4(p):
        r = ORDER[p]
        for j in (1, 3, 2):
            arrived("y2", r, j - 1)
        mine = hid.at[r, pl.ds(c * NY, NY)]
        send(("c2", r), mine, mine, sibling)

    def op_s5(p):
        r = ORDER[p]
        if p == 0:
            loads[4].wait()
        arrived("c2", r)
        h = hid[r].reshape(CHUNK, ff)

        for n in range(wd.shape[1] // 256):
            cols = pl.ds(n * 256, 256)
            out = jnp.dot(h, wd[:, cols], preferred_element_type=F32).reshape(NX, OWN, 256)
            x_own[r, :, :, cols] = out
            x_out[r, :, :, cols] = out.astype(BF16)

        for j in (2, 1, 3):
            send(("x2", r, j - 1), x_out.at[r, (x + j) % NX], x_in.at[r, j - 1], x_peer[j])
        hid_t[:, pl.ds(r * CHUNK, CHUNK)] = h.T

    def op_s6(p):
        r = ORDER[p]
        total = x_own[r, x]
        for j in (1, 3, 2):
            arrived("x2", r, j - 1)
            total = total + x_in[r, j - 1].astype(F32)
        if r == 0:
            x_own[0, x] = total
        else:
            z_out[r] = total.astype(BF16)
            send(("z2", r), z_out.at[r], z_in.at[r], z_peer[r])

    def op_grad(n):
        cols = pl.ds(n * 256, 256)
        down_grad[:, cols] = jnp.dot(
            hid_t[...], og[:, :, :, cols].reshape(NZ * CHUNK, 256), preferred_element_type=F32)

    def op_s7():
        for key, (src, _) in started.items():
            copy(key, src, src, sibling).wait_send()
        total = x_own[0, x]
        for r in ORDER[1:]:
            arrived("z2", r)
            total = total + z_in[r].astype(F32)
        mixed[...] = total.astype(BF16)

    ops = {"zs": op_zs, "tokr": op_tokr, "og_start": op_og_start, "ogs": op_ogs, "s1": op_s1, "s2": op_s2, "s3": op_s3, "s4": op_s4,
           "s5": op_s5, "s6": op_s6, "grad": op_grad, "s7": op_s7}
    for op in schedule():
        ops[op[0]](*op[1:])


def finish(mixed, down_grad, mixed_out, down_grad_out, sem):
    copies = [
        pltpu.make_async_copy(mixed, mixed_out, sem.at[0]),
        pltpu.make_async_copy(down_grad, down_grad_out, sem.at[1]),
    ]
    for copy in copies:
        copy.start()
    for copy in copies:
        copy.wait()


SEMS = {
    "zt": (NZ,), "xt": (NZ, NX - 1), "c1": (NZ, 2), "y1": (NZ, NY - 1), "y2": (NZ, NY - 1),
    "c2": (NZ,), "x2": (NZ, NX - 1), "z2": (NZ,), "ox": (NX - 1,), "oz": (NZ,),
}


def local(tokens, gate_w, up_w, down_w, out_grad):
    d, ff = gate_w.shape
    dma = pltpu.SemaphoreType.DMA
    vmem, hbm = pl.BlockSpec(memory_space=pltpu.VMEM), pl.BlockSpec(memory_space=pltpu.HBM)
    mixed, down_grad = pl.pallas_call(
        kernel,
        out_shape=(
            pltpu.VMEM((OWN, d), BF16),
            pltpu.VMEM((ff, d), F32),
        ),
        in_specs=[hbm] * 5,
        out_specs=(vmem, vmem),
        scratch_shapes=[
            pltpu.VMEM((d, 2 * ff), BF16),
            pltpu.VMEM((ff, d), BF16),
            pltpu.VMEM((NZ, NX, OWN, d), BF16),
            pltpu.VMEM((NZ, NX, OWN, d), BF16),
            pltpu.VMEM((NZ, 2, NY, PART, 2 * ff), F32),
            pltpu.VMEM((NZ, NY, PART, 2 * ff), F32),
            pltpu.VMEM((NZ, NY - 1, PART, 2 * ff), BF16),
            pltpu.VMEM((NZ, NY - 1, PART, 2 * ff), BF16),
            pltpu.VMEM((NZ, 2 * NY, PART, ff), BF16),
            pltpu.VMEM((ff, NZ * CHUNK), BF16),
            pltpu.VMEM((NZ, NX, OWN, d), F32),
            pltpu.VMEM((NZ, NX, OWN, d), BF16),
            pltpu.VMEM((NZ, NX - 1, OWN, d), BF16),
            pltpu.VMEM((NZ, OWN, d), BF16),
            pltpu.VMEM((NZ, OWN, d), BF16),
            dma((5,)),
            *[dma(shape) for shape in SEMS.values() for _ in range(2)],
        ],
        compiler_params=pltpu.CompilerParams(
            collective_id=0, has_side_effects=True, vmem_limit_bytes=42 * 2**20),
        cost_estimate=pl.CostEstimate(flops=7_600_000_000, bytes_accessed=10_000_000, transcendentals=120_000),
    )(*[pltpu.with_memory_space_constraint(a, pltpu.HBM) for a in (tokens, gate_w, up_w, down_w, out_grad)])
    return pl.pallas_call(
        finish,
        out_shape=(
            jax.ShapeDtypeStruct((OWN, d), BF16),
            jax.ShapeDtypeStruct((ff, d), F32),
        ),
        in_specs=[vmem, vmem],
        out_specs=(hbm, hbm),
        scratch_shapes=[dma((2,))],
        compiler_params=pltpu.CompilerParams(vmem_limit_bytes=2**20),
    )(*[pltpu.with_memory_space_constraint(a, pltpu.VMEM) for a in (mixed, down_grad)])


def solution(mesh):
    return jax.shard_map(
        local,
        mesh=mesh,
        in_specs=(P("col", "row"), P("row", "col"), P("row", "col"), P("col", "row"), P("col", "row")),
        out_specs=(P("col", "row"), P("col", "row")),
        check_vma=False,
    )
```
